32 devices in a mesh: parts: 2 (over y), pair: 16 (over z, x, core).
Axes of the slice: x: 2, y: 2, z: 4, core: 2. Of those that a mesh axis runs over, the one named last changes fastest.
Arguments:
- amplitudes: bfloat16 [32, 8192], P(('parts', 'pair')), parts along dimension 0, may hold values from -6 to 6
- tile_counts: int32 [32], P('parts'), parts along dimension 0, may hold values from 1 to 8, 64 in all
- screen: int32 [256, 16], P(('parts', 'pair')), parts along dimension 0, may hold values from 0 to 23
- ladder_ints: bfloat16 [256, 16, 128, 128], P(('parts', 'pair')), parts along dimension 0, may hold values from -0.125 to 0.125
- hole_ints: bfloat16 [32, 16], P(('parts', 'pair')), parts along dimension 0, may hold values from -1.5 to 1.5
- direct: bfloat16 [32, 8192], P(('parts', 'pair')), parts along dimension 0, may hold values from -6 to 6
- occ_energy: float32 [32], P(('parts', 'pair')), parts along dimension 0, may hold values from -3 to -0.5
- virt_energy: float32 [16384], P('parts'), parts along dimension 0, may hold values from 0.5 to 4
Outputs:
- updated: float32 [32, 8192], P(('parts', 'pair')), parts along dimension 0
The draws below stay inside these ranges and needn't reach their ends.
There are 2 independent parts, one for each index of `parts`. The reference program is written for one: setup_inputs(seed, part) draws one part's arguments, and reference() takes and returns one part's arrays. A program takes and returns all parts, laid end to end along the dimension named above; each array names one. Nothing has to cross between parts.
Inputs may be any that keep to these rules, and one draw needn't show every extreme that they name: `tile_counts`: owner counts sum to 64, and the largest is 8. `screen`: an entry names an extended slot of the owner of its row's tile; it may name an empty slot.
All inputs are finite; a program needn't handle non-finite values.
Results may differ from the reference program's by a relative error of at most 0.0045.
Values may be sent and summed in bfloat16 or wider, within the bound.
A program may use at most 64 MiB of HBM per device.

```python
import math
import jax
import jax.numpy as jnp
import numpy as np
from jax import lax

TILE = 128
NQ = 16
CAP = 8
NO = 16
NT = 64
N_PAIR = 16


def place_ends(array, stream_key, low, largest):
    spot = [jax.random.randint(jax.random.fold_in(stream_key, axis), (), 0, length) for axis, length in enumerate(array.shape)]
    widest = array.shape.index(max(array.shape))
    beside = spot[:widest] + [(spot[widest] + 1) % array.shape[widest]] + spot[widest + 1:]
    return array.at[tuple(spot)].set(low).at[tuple(beside)].set(largest)


def shard_levels(own_key, dims, split, low, top_value):
    level, own = 1.0, jax.random.fold_in(own_key, 6)
    for axis_at, parts in split:
        steps = jnp.exp(jax.random.uniform(jax.random.fold_in(own, axis_at), (parts,), jnp.float32, low / len(split), top_value / len(split)))
        level = level * jnp.repeat(steps, dims[axis_at] // parts).reshape([-1 if axis == axis_at else 1 for axis in range(len(dims))])
    return level


def profile(number_of, total, bound, lean):
    portions = [(1 << 20) // math.isqrt(rank ** lean) + 1 for rank in range(2, number_of + 1)]
    spare, given = total - bound - (number_of - 1), [1] * (number_of - 1)
    while spare > 0:
        candidates = [i for i in range(number_of - 1) if given[i] < bound]
        pool, remaining = sum([portions[i] for i in candidates]), spare
        for i in candidates:
            addition = min(bound - given[i], max(1, remaining * portions[i] // pool), spare)
            given[i] = given[i] + addition
            spare = spare - addition
    return np.array([bound] + given)


def ragged(own_key, count, total, reach, slope):
    if count == 2:
        one = jax.random.randint(own_key, (), max(1, total - reach), min(reach, total - 1) + 1)
        return jnp.stack([one, total - one])
    lengths = jnp.asarray(profile(count, total, reach, slope), jnp.int32)
    pairs = (count - 1) // 2
    donor, receiver = lengths[1:1 + 2 * pairs:2], lengths[2:2 + 2 * pairs:2]
    margin = jnp.minimum(donor - 1, reach - receiver)
    passed = jax.random.randint(jax.random.fold_in(own_key, 1), (pairs,), 0, 1 << 20) % (margin + 1)
    lengths = lengths.at[1:1 + 2 * pairs:2].set(donor - passed).at[2:2 + 2 * pairs:2].set(receiver + passed)
    return lengths[jax.random.permutation(jax.random.fold_in(own_key, 2), count)]


def normal_values(rng, dims, width, reach, split=(), kind=jnp.bfloat16):
    result = width * jax.random.normal(rng, dims, jnp.float32)
    if split:
        result = result * shard_levels(rng, dims, split, -0.22, 0.18)
    return jnp.clip(result, -reach, reach).astype(kind)


def setup_inputs(seed: int = 0, part: int = 0) -> dict:
    key_of = jax.random.split(jax.random.key(seed), 9)
    part_keys = jax.random.split(jax.random.fold_in(key_of[8], part), 9)
    return {
        "amplitudes": normal_values(part_keys[0], (NO, NT * TILE), 1.0, 6.0, ((0, 16),)),
        "tile_counts": ragged(part_keys[1], N_PAIR, NT, CAP, 2).astype(jnp.int32),
        "screen": place_ends(jax.random.randint(part_keys[2], (N_PAIR * CAP, NQ), 0, 3 * CAP), jax.random.fold_in(part_keys[2], 1), 0, (3 * CAP) - 1).astype(jnp.int32),
        "ladder_ints": normal_values(part_keys[3], (N_PAIR * CAP, NQ, TILE, TILE), (NQ * TILE) ** -0.5, 0.125, ((0, 16),)),
        "hole_ints": normal_values(part_keys[4], (NO, NO), NO ** -0.5, 1.5, ((0, 16),)),
        "direct": normal_values(part_keys[5], (NO, NT * TILE), 1.0, 6.0, ((0, 16),)),
        "occ_energy": jnp.clip(-3.0 + 2.5 * jax.random.uniform(part_keys[6], (NO,), jnp.float32) ** shard_levels(part_keys[6], (NO,), ((0, 16),), -0.2, 0.2), -3.0, -0.5),
        "virt_energy": jnp.clip(jax.random.uniform(part_keys[7], (NT * TILE,), jnp.float32, 0.5, 4.0), 0.5, 4.0),
    }


def reference(amplitudes, tile_counts, screen, ladder_ints, hole_ints, direct, occ_energy, virt_energy):
    rows_all = amplitudes.shape[0]
    counts = tile_counts.astype(jnp.int32)
    offsets = (jnp.cumsum(counts) - counts).astype(jnp.int32)
    by_tile = amplitudes.reshape(rows_all, NT, TILE)
    positions = jnp.arange(NT, dtype=jnp.int32)
    owner_of = (jnp.sum((offsets[None, :] <= positions[:, None]).astype(jnp.int32), axis=1) - 1).astype(jnp.int32)
    slot_of = (positions - offsets[owner_of]).astype(jnp.int32)

    def one_tile(operands):
        owner, slot = operands
        row_index = (owner * CAP + slot).astype(jnp.int32)
        chosen = screen[row_index].astype(jnp.int32)
        neighbour = ((owner - 1 + chosen // CAP) % N_PAIR).astype(jnp.int32)
        within = (chosen % CAP).astype(jnp.int32)
        live = within < counts[neighbour]
        source = jnp.minimum(offsets[neighbour] + within, NT - 1).astype(jnp.int32)
        picked = jnp.take(by_tile, source, axis=1)
        picked = jnp.where(live[None, :, None], picked, jnp.zeros_like(picked))
        blocks = ladder_ints[row_index]
        return jnp.dot(picked.reshape(rows_all, NQ * TILE), blocks.reshape(NQ * TILE, TILE), preferred_element_type=jnp.float32)

    ladder_tiles = lax.map(one_tile, (owner_of, slot_of))
    ladder_term = jnp.transpose(ladder_tiles, (1, 0, 2)).reshape(rows_all, NT * TILE)
    hole_term = jnp.dot(hole_ints, amplitudes, preferred_element_type=jnp.float32)
    coupled = (ladder_term + hole_term).astype(jnp.bfloat16)
    summed = direct.astype(jnp.float32) + coupled.astype(jnp.float32)
    denominator = virt_energy[None, :] - occ_energy[:, None]
    return summed / denominator
```

```python
import functools

import jax
import jax.numpy as jnp
from jax import lax
from jax.experimental import pallas as pl
from jax.experimental.pallas import tpu as pltpu
from jax.sharding import PartitionSpec as P

TILE = 128
CAP = 8
MSG = 32
F32 = jnp.float32
BF16 = jnp.bfloat16


def each(count, body):
    if count <= 64:
        for i in range(count):
            body(i)
    else:
        def step(i, carry):
            body(i)
            return carry

        lax.fori_loop(0, count, step, 0)


def kernel(
    n,
    nt,
    nq,
    counts,
    screen,
    occ,
    amp_hbm,
    hole_hbm,
    ladder_hbm,
    direct_hbm,
    virt_hbm,
    out,
    amp_v,
    hole_v,
    ladder_v,
    direct_v,
    virt_v,
    tiles,
    direct_t,
    onehot,
    onehot_t,
    owned,
    send1,
    recv1,
    recv1_f,
    ext,
    coupled,
    send2,
    recv2,
    in_sem,
    ladder_sem,
    send1_sem,
    recv1_sem,
    send2_sem,
    recv2_sem,
):
    me = lax.axis_index("pair")
    cols = onehot.shape[1]

    copy_amp = pltpu.make_async_copy(amp_hbm, amp_v, in_sem.at[0])
    copy_hole = pltpu.make_async_copy(hole_hbm, hole_v, in_sem.at[1])
    copy_direct = pltpu.make_async_copy(direct_hbm, direct_v, in_sem.at[2])
    copy_virt = pltpu.make_async_copy(virt_hbm, virt_v, in_sem.at[3])
    copy_amp.start()
    copy_hole.start()

    barrier = pltpu.get_barrier_semaphore()

    def greet(t):
        pl.semaphore_signal(
            barrier, inc=1, device_id={"pair": lax.rem(me + 1 + t, n)}
        )

    each(n - 1, greet)

    ladder_copies = [
        pltpu.make_async_copy(ladder_hbm.at[s], ladder_v.at[s], ladder_sem.at[s])
        for s in range(CAP)
    ]
    for copy in ladder_copies:
        copy.start()
    copy_direct.start()
    copy_virt.start()

    lane = lax.broadcasted_iota(jnp.int32, (CAP, cols), 1)
    slot = lax.broadcasted_iota(jnp.int32, (CAP, cols), 0)

    def mark(e, offset):
        count = counts[e]
        hit = jnp.logical_and(lane == slot + offset, slot < count)
        row = e * CAP if isinstance(e, int) else pl.multiple_of(e * CAP, CAP)
        onehot[pl.ds(row, CAP), :] = jnp.where(hit, 1.0, 0.0).astype(F32)
        return offset + count

    if n <= 64:
        offset = jnp.int32(0)
        for e in range(n):
            offset = mark(e, offset)
    else:
        lax.fori_loop(0, n, mark, jnp.int32(0))

    copy_amp.wait()
    copy_hole.wait()
    tiles[pl.ds(nt, cols - nt), :] = jnp.zeros((cols - nt, TILE), F32)

    def lay(source, target):
        def body(t):
            at = t * TILE if isinstance(t, int) else pl.multiple_of(t * TILE, TILE)
            target[pl.ds(t, 1), :] = source[:, pl.ds(at, TILE)].astype(F32)

        each(nt, body)

    lay(amp_v, tiles)
    owned[...] = jnp.dot(
        onehot[...].astype(BF16), tiles[...].astype(BF16), preferred_element_type=F32
    )
    hole_row = jnp.concatenate(
        [hole_v[...].astype(F32), jnp.zeros((1, TILE - n), F32)], axis=1
    ) if n < TILE else hole_v[...].astype(F32)
    first = lax.broadcasted_iota(jnp.int32, (CAP, TILE), 0) == 0
    hole_block = jnp.where(first, jnp.broadcast_to(hole_row, (CAP, TILE)), 0.0)

    def compose(d):
        def block(e):
            row = e * CAP if isinstance(e, int) else pl.multiple_of(e * CAP, CAP)
            return owned[pl.ds(row, CAP), :]

        if isinstance(d, int):
            low, high = (d - 1) % n, (d + 1) % n
        else:
            low, high = lax.rem(d + n - 1, n), lax.rem(d + 1, n)
        send1[d] = jnp.concatenate(
            [block(low), block(d), block(high), hole_block], axis=0
        ).astype(BF16)

    each(n, compose)

    pl.semaphore_wait(barrier, n - 1)

    def to_owner(t):
        d = lax.rem(me + 1 + t, n)
        pltpu.make_async_remote_copy(
            src_ref=send1.at[d],
            dst_ref=recv1.at[me],
            send_sem=send1_sem,
            recv_sem=recv1_sem,
            device_id={"pair": d},
        ).start()

    each(n - 1, to_owner)
    recv1[me] = send1[me]

    onehot_t[...] = onehot[...].T.astype(BF16)
    copy_direct.wait()
    copy_virt.wait()
    lay(direct_v, direct_t)

    def everything(send, recv, send_sem, recv_sem):
        return pltpu.make_async_remote_copy(
            src_ref=send.at[pl.ds(0, n - 1)],
            dst_ref=recv.at[pl.ds(0, n - 1)],
            send_sem=send_sem,
            recv_sem=recv_sem,
            device_id={"pair": lax.rem(me + 1, n)},
        )

    everything(send1, recv1, send1_sem, recv1_sem).wait_recv()

    recv1_f[...] = recv1[...].astype(F32).reshape(n * MSG, TILE)
    for j in range(3 * CAP):
        ext[j] = recv1_f[pl.ds(j, n, stride=MSG), :].astype(BF16)
    holes = recv1_f[pl.ds(3 * CAP, n, stride=MSG), :][:, :n].astype(BF16)

    for s in range(CAP):
        ladder_copies[s].wait()
        picked = jnp.concatenate([ext[screen[s, k]] for k in range(nq)], axis=1)
        ladder = jnp.dot(picked, ladder_v[s], preferred_element_type=F32)
        hole = jnp.dot(holes, ext[CAP + s], preferred_element_type=F32)
        coupled[pl.ds(s * n, n), :] = ladder + hole

    def to_row(t):
        d = lax.rem(me + 1 + t, n)
        pltpu.make_async_remote_copy(
            src_ref=send2.at[d],
            dst_ref=recv2.at[me],
            send_sem=send2_sem,
            recv_sem=recv2_sem,
            device_id={"pair": d},
        ).start()

    def split(i):
        send2[i] = coupled[pl.ds(i, CAP, stride=n), :]

    each(n, split)
    each(n - 1, to_row)
    recv2[me] = send2[me]
    everything(send2, recv2, send2_sem, recv2_sem).wait_recv()

    home = recv2[...].reshape(n * CAP, TILE).astype(BF16)
    sums = jnp.dot(onehot_t[...], home, preferred_element_type=F32)[:nt]
    out[...] = (direct_t[...] + sums) / (virt_v[...] - occ[0])
    everything(send1, recv1, send1_sem, recv1_sem).wait_send()
    everything(send2, recv2, send2_sem, recv2_sem).wait_send()


def shards(
    amplitudes, tile_counts, screen, ladder_ints, hole_ints, direct, occ_energy, virt_energy
):
    n = lax.axis_size("pair")
    nt = amplitudes.shape[1] // TILE
    nq = screen.shape[1]
    cols = -(-nt // TILE) * TILE
    if cols == nt:
        cols += TILE
    smem = pl.BlockSpec(memory_space=pltpu.SMEM)
    hbm = pl.BlockSpec(memory_space=pl.ANY)
    updated = pl.pallas_call(
        functools.partial(kernel, n, nt, nq),
        out_shape=jax.ShapeDtypeStruct((nt, TILE), F32),
        in_specs=[smem, smem, smem, hbm, hbm, hbm, hbm, hbm],
        out_specs=pl.BlockSpec(memory_space=pltpu.VMEM),
        scratch_shapes=[
            pltpu.VMEM((1, nt * TILE), BF16),
            pltpu.VMEM((1, n), BF16),
            pltpu.VMEM((CAP, nq * TILE, TILE), BF16),
            pltpu.VMEM((1, nt * TILE), BF16),
            pltpu.VMEM((nt, TILE), F32),
            pltpu.VMEM((cols, TILE), F32),
            pltpu.VMEM((nt, TILE), F32),
            pltpu.VMEM((n * CAP, cols), F32),
            pltpu.VMEM((cols, n * CAP), BF16),
            pltpu.VMEM((n * CAP, TILE), F32),
            pltpu.VMEM((n, MSG, TILE), BF16),
            pltpu.VMEM((n, MSG, TILE), BF16),
            pltpu.VMEM((n * MSG, TILE), F32),
            pltpu.VMEM((3 * CAP, n, TILE), BF16),
            pltpu.VMEM((CAP * n, TILE), F32),
            pltpu.VMEM((n, CAP, TILE), F32),
            pltpu.VMEM((n, CAP, TILE), F32),
            pltpu.SemaphoreType.DMA((4,)),
            pltpu.SemaphoreType.DMA((CAP,)),
            pltpu.SemaphoreType.DMA,
            pltpu.SemaphoreType.DMA,
            pltpu.SemaphoreType.DMA,
            pltpu.SemaphoreType.DMA,
        ],
        compiler_params=pltpu.CompilerParams(
            collective_id=0, has_side_effects=True, vmem_limit_bytes=48 * 1024 * 1024
        ),
        cost_estimate=pl.CostEstimate(
            flops=2 * CAP * nq * TILE * TILE * n,
            bytes_accessed=CAP * nq * TILE * TILE * 2,
            transcendentals=0,
        ),
    )(
        tile_counts,
        screen,
        occ_energy,
        amplitudes,
        hole_ints,
        ladder_ints.reshape(CAP, nq * TILE, TILE),
        direct,
        virt_energy.reshape(nt, TILE),
    )
    return updated.reshape(1, nt * TILE)


def solution(mesh):
    return jax.shard_map(
        shards,
        mesh=mesh,
        in_specs=(
            P(("parts", "pair"), None),
            P("parts"),
            P(("parts", "pair"), None),
            P(("parts", "pair"), None, None, None),
            P(("parts", "pair"), None),
            P(("parts", "pair"), None),
            P(("parts", "pair")),
            P("parts"),
        ),
        out_specs=P(("parts", "pair"), None),
        check_vma=False,
    )
```

```python
import functools

import jax
import jax.numpy as jnp
from jax import lax
from jax.experimental import pallas as pl
from jax.experimental.pallas import tpu as pltpu
from jax.sharding import PartitionSpec as P

TILE = 128
CAP = 8
MSG = 32
F32 = jnp.float32
BF16 = jnp.bfloat16


def each(count, body):
    if count <= 64:
        for i in range(count):
            body(i)
    else:
        def step(i, carry):
            body(i)
            return carry

        lax.fori_loop(0, count, step, 0)


def kernel(
    n,
    nt,
    nq,
    counts_hbm,
    screen_hbm,
    occ_hbm,
    amp_hbm,
    hole_hbm,
    ladder_hbm,
    direct_hbm,
    virt_hbm,
    out,
    counts,
    screen,
    occ,
    amp_v,
    hole_v,
    ladder_v,
    direct_v,
    virt_v,
    tiles,
    direct_t,
    onehot,
    onehot_t,
    owned,
    send1,
    recv1,
    recv1_f,
    ext,
    coupled,
    send2,
    recv2,
    in_sem,
    ladder_sem,
    send1_sem,
    recv1_sem,
    send2_sem,
    recv2_sem,
):
    me = lax.axis_index("pair")
    cols = onehot.shape[1]

    copy_amp = pltpu.make_async_copy(amp_hbm, amp_v, in_sem.at[0])
    copy_hole = pltpu.make_async_copy(hole_hbm, hole_v, in_sem.at[1])
    copy_direct = pltpu.make_async_copy(direct_hbm, direct_v, in_sem.at[2])
    copy_virt = pltpu.make_async_copy(virt_hbm, virt_v, in_sem.at[3])
    copy_counts = pltpu.make_async_copy(counts_hbm, counts, in_sem.at[4])
    copy_screen = pltpu.make_async_copy(screen_hbm, screen, in_sem.at[5])
    copy_occ = pltpu.make_async_copy(occ_hbm, occ, in_sem.at[6])
    copy_counts.start()
    copy_amp.start()
    copy_hole.start()

    barrier = pltpu.get_barrier_semaphore()

    def greet(t):
        pl.semaphore_signal(
            barrier, inc=1, device_id={"pair": lax.rem(me + 1 + t, n)}
        )

    each(n - 1, greet)

    ladder_copies = [
        pltpu.make_async_copy(ladder_hbm.at[s], ladder_v.at[s], ladder_sem.at[s])
        for s in range(CAP)
    ]
    for copy in ladder_copies:
        copy.start()
    copy_screen.start()
    copy_direct.start()
    copy_virt.start()
    copy_occ.start()

    lane = lax.broadcasted_iota(jnp.int32, (CAP, cols), 1)
    slot = lax.broadcasted_iota(jnp.int32, (CAP, cols), 0)

    def mark(e, offset):
        count = counts[e]
        hit = jnp.logical_and(lane == slot + offset, slot < count)
        row = e * CAP if isinstance(e, int) else pl.multiple_of(e * CAP, CAP)
        onehot[pl.ds(row, CAP), :] = jnp.where(hit, 1.0, 0.0).astype(F32)
        return offset + count

    copy_counts.wait()
    if n <= 64:
        offset = jnp.int32(0)
        for e in range(n):
            offset = mark(e, offset)
    else:
        lax.fori_loop(0, n, mark, jnp.int32(0))

    copy_amp.wait()
    copy_hole.wait()
    tiles[pl.ds(nt, cols - nt), :] = jnp.zeros((cols - nt, TILE), F32)

    def lay(source, target):
        def body(t):
            at = t * TILE if isinstance(t, int) else pl.multiple_of(t * TILE, TILE)
            target[pl.ds(t, 1), :] = source[:, pl.ds(at, TILE)].astype(F32)

        each(nt, body)

    lay(amp_v, tiles)
    owned[...] = jnp.dot(
        onehot[...].astype(BF16), tiles[...].astype(BF16), preferred_element_type=F32
    )
    hole_row = jnp.concatenate(
        [hole_v[...].astype(F32), jnp.zeros((1, TILE - n), F32)], axis=1
    ) if n < TILE else hole_v[...].astype(F32)
    first = lax.broadcasted_iota(jnp.int32, (CAP, TILE), 0) == 0
    hole_block = jnp.where(first, jnp.broadcast_to(hole_row, (CAP, TILE)), 0.0)

    def compose(d):
        def block(e):
            row = e * CAP if isinstance(e, int) else pl.multiple_of(e * CAP, CAP)
            return owned[pl.ds(row, CAP), :]

        if isinstance(d, int):
            low, high = (d - 1) % n, (d + 1) % n
        else:
            low, high = lax.rem(d + n - 1, n), lax.rem(d + 1, n)
        send1[d] = jnp.concatenate(
            [block(low), block(d), block(high), hole_block], axis=0
        ).astype(BF16)

    each(n, compose)

    pl.semaphore_wait(barrier, n - 1)

    def to_owner(t):
        d = lax.rem(me + 1 + t, n)
        pltpu.make_async_remote_copy(
            src_ref=send1.at[d],
            dst_ref=recv1.at[me],
            send_sem=send1_sem,
            recv_sem=recv1_sem,
            device_id={"pair": d},
        ).start()

    each(n - 1, to_owner)
    recv1[me] = send1[me]

    onehot_t[...] = onehot[...].T.astype(BF16)
    copy_direct.wait()
    copy_virt.wait()
    copy_screen.wait()
    copy_occ.wait()
    lay(direct_v, direct_t)

    def everything(send, recv, send_sem, recv_sem):
        return pltpu.make_async_remote_copy(
            src_ref=send.at[pl.ds(0, n - 1)],
            dst_ref=recv.at[pl.ds(0, n - 1)],
            send_sem=send_sem,
            recv_sem=recv_sem,
            device_id={"pair": lax.rem(me + 1, n)},
        )

    everything(send1, recv1, send1_sem, recv1_sem).wait_recv()

    recv1_f[...] = recv1[...].astype(F32).reshape(n * MSG, TILE)
    for j in range(3 * CAP):
        ext[j] = recv1_f[pl.ds(j, n, stride=MSG), :].astype(BF16)
    holes = recv1_f[pl.ds(3 * CAP, n, stride=MSG), :][:, :n].astype(BF16)

    for s in range(CAP):
        ladder_copies[s].wait()
        picked = jnp.concatenate([ext[screen[s, k]] for k in range(nq)], axis=1)
        ladder = jnp.dot(picked, ladder_v[s], preferred_element_type=F32)
        hole = jnp.dot(holes, ext[CAP + s], preferred_element_type=F32)
        coupled[pl.ds(s * n, n), :] = ladder + hole

    def to_row(t):
        d = lax.rem(me + 1 + t, n)
        pltpu.make_async_remote_copy(
            src_ref=send2.at[d],
            dst_ref=recv2.at[me],
            send_sem=send2_sem,
            recv_sem=recv2_sem,
            device_id={"pair": d},
        ).start()

    def split(i):
        send2[i] = coupled[pl.ds(i, CAP, stride=n), :]

    each(n, split)
    each(n - 1, to_row)
    recv2[me] = send2[me]
    everything(send2, recv2, send2_sem, recv2_sem).wait_recv()

    home = recv2[...].reshape(n * CAP, TILE).astype(BF16)
    sums = jnp.dot(onehot_t[...], home, preferred_element_type=F32)[:nt]
    out[...] = (direct_t[...] + sums) / (virt_v[...] - occ[0])
    everything(send1, recv1, send1_sem, recv1_sem).wait_send()
    everything(send2, recv2, send2_sem, recv2_sem).wait_send()


def shards(
    amplitudes, tile_counts, screen, ladder_ints, hole_ints, direct, occ_energy, virt_energy
):
    n = lax.axis_size("pair")
    nt = amplitudes.shape[1] // TILE
    nq = screen.shape[1]
    cols = -(-nt // TILE) * TILE
    if cols == nt:
        cols += TILE
    hbm = pl.BlockSpec(memory_space=pltpu.HBM)
    updated = pl.pallas_call(
        functools.partial(kernel, n, nt, nq),
        out_shape=jax.ShapeDtypeStruct((nt, TILE), F32),
        in_specs=[hbm] * 8,
        out_specs=pl.BlockSpec(memory_space=pltpu.VMEM),
        scratch_shapes=[
            pltpu.SMEM((n,), jnp.int32),
            pltpu.SMEM((CAP, nq), jnp.int32),
            pltpu.SMEM((1,), F32),
            pltpu.VMEM((1, nt * TILE), BF16),
            pltpu.VMEM((1, n), BF16),
            pltpu.VMEM((CAP, nq * TILE, TILE), BF16),
            pltpu.VMEM((1, nt * TILE), BF16),
            pltpu.VMEM((nt, TILE), F32),
            pltpu.VMEM((cols, TILE), F32),
            pltpu.VMEM((nt, TILE), F32),
            pltpu.VMEM((n * CAP, cols), F32),
            pltpu.VMEM((cols, n * CAP), BF16),
            pltpu.VMEM((n * CAP, TILE), F32),
            pltpu.VMEM((n, MSG, TILE), BF16),
            pltpu.VMEM((n, MSG, TILE), BF16),
            pltpu.VMEM((n * MSG, TILE), F32),
            pltpu.VMEM((3 * CAP, n, TILE), BF16),
            pltpu.VMEM((CAP * n, TILE), F32),
            pltpu.VMEM((n, CAP, TILE), F32),
            pltpu.VMEM((n, CAP, TILE), F32),
            pltpu.SemaphoreType.DMA((7,)),
            pltpu.SemaphoreType.DMA((CAP,)),
            pltpu.SemaphoreType.DMA,
            pltpu.SemaphoreType.DMA,
            pltpu.SemaphoreType.DMA,
            pltpu.SemaphoreType.DMA,
        ],
        compiler_params=pltpu.CompilerParams(
            collective_id=0, has_side_effects=True, vmem_limit_bytes=62 * 1024 * 1024
        ),
        cost_estimate=pl.CostEstimate(
            flops=2 * CAP * nq * TILE * TILE * n,
            bytes_accessed=CAP * nq * TILE * TILE * 2,
            transcendentals=0,
        ),
    )(
        tile_counts,
        screen,
        occ_energy,
        amplitudes,
        hole_ints,
        ladder_ints.reshape(CAP, nq * TILE, TILE),
        direct,
        virt_energy.reshape(nt, TILE),
    )
    return updated.reshape(1, nt * TILE)


def solution(mesh):
    return jax.shard_map(
        shards,
        mesh=mesh,
        in_specs=(
            P(("parts", "pair"), None),
            P("parts"),
            P(("parts", "pair"), None),
            P(("parts", "pair"), None, None, None),
            P(("parts", "pair"), None),
            P(("parts", "pair"), None),
            P(("parts", "pair")),
            P("parts"),
        ),
        out_specs=P(("parts", "pair"), None),
        check_vma=False,
    )
```

```python
import functools

import jax
import jax.numpy as jnp
from jax import lax
from jax.experimental import pallas as pl
from jax.experimental.pallas import tpu as pltpu
from jax.sharding import PartitionSpec as P

TILE = 128
CAP = 8
GROUP = 4
MSG = 32
F32 = jnp.float32
BF16 = jnp.bfloat16


def each(count, body):
    if count <= 64:
        for i in range(count):
            body(i)
    else:
        def step(i, carry):
            body(i)
            return carry

        lax.fori_loop(0, count, step, 0)


def far_first(n):
    if n % GROUP or n > 64:
        return None
    groups = n // GROUP
    ends = []
    for far in range(1, groups // 2 + 1):
        ends.append([groups - far] if 2 * far == groups else [groups - far, far])
    steps = [(far, near) for pair in ends for near in range(GROUP) for far in pair]
    return steps + [(0, near) for near in range(1, GROUP)]


def kernel(
    n,
    nt,
    nq,
    counts_hbm,
    screen_hbm,
    occ_hbm,
    amp_hbm,
    hole_hbm,
    ladder_hbm,
    direct_hbm,
    virt_hbm,
    out,
    counts,
    screen,
    occ,
    amp_v,
    hole_v,
    ladder_v,
    direct_v,
    virt_v,
    tiles,
    direct_t,
    onehot,
    onehot_t,
    owned,
    send1,
    recv1,
    recv1_f,
    ext,
    coupled,
    send2,
    recv2,
    in_sem,
    ladder_sem,
    send1_sem,
    recv1_sem,
    send2_sem,
    recv2_sem,
):
    me = lax.axis_index("pair")
    cols = onehot.shape[1]
    steps = far_first(n)

    def to_peers(body):
        if steps is None:
            each(n - 1, lambda t: body(lax.rem(me + 1 + t, n)))
        else:
            for far, near in steps:
                group = lax.rem(me // GROUP + far, n // GROUP)
                body(group * GROUP + lax.rem(me + near, GROUP))

    copy_amp = pltpu.make_async_copy(amp_hbm, amp_v, in_sem.at[0])
    copy_hole = pltpu.make_async_copy(hole_hbm, hole_v, in_sem.at[1])
    copy_direct = pltpu.make_async_copy(direct_hbm, direct_v, in_sem.at[2])
    copy_virt = pltpu.make_async_copy(virt_hbm, virt_v, in_sem.at[3])
    copy_counts = pltpu.make_async_copy(counts_hbm, counts, in_sem.at[4])
    copy_screen = pltpu.make_async_copy(screen_hbm, screen, in_sem.at[5])
    copy_occ = pltpu.make_async_copy(occ_hbm, occ, in_sem.at[6])
    copy_counts.start()
    copy_amp.start()
    copy_hole.start()

    barrier = pltpu.get_barrier_semaphore()

    def greet(t):
        pl.semaphore_signal(
            barrier, inc=1, device_id={"pair": lax.rem(me + 1 + t, n)}
        )

    each(n - 1, greet)

    ladder_copies = [
        pltpu.make_async_copy(ladder_hbm.at[s], ladder_v.at[s], ladder_sem.at[s])
        for s in range(CAP)
    ]
    for copy in ladder_copies:
        copy.start()
    copy_screen.start()
    copy_direct.start()
    copy_virt.start()
    copy_occ.start()

    lane = lax.broadcasted_iota(jnp.int32, (CAP, cols), 1)
    slot = lax.broadcasted_iota(jnp.int32, (CAP, cols), 0)

    def mark(e, offset):
        count = counts[e]
        hit = jnp.logical_and(lane == slot + offset, slot < count)
        row = e * CAP if isinstance(e, int) else pl.multiple_of(e * CAP, CAP)
        onehot[pl.ds(row, CAP), :] = jnp.where(hit, 1.0, 0.0).astype(F32)
        return offset + count

    copy_counts.wait()
    if n <= 64:
        offset = jnp.int32(0)
        for e in range(n):
            offset = mark(e, offset)
    else:
        lax.fori_loop(0, n, mark, jnp.int32(0))

    copy_amp.wait()
    copy_hole.wait()
    tiles[pl.ds(nt, cols - nt), :] = jnp.zeros((cols - nt, TILE), F32)

    def lay(source, target):
        def body(t):
            at = t * TILE if isinstance(t, int) else pl.multiple_of(t * TILE, TILE)
            target[pl.ds(t, 1), :] = source[:, pl.ds(at, TILE)].astype(F32)

        each(nt, body)

    lay(amp_v, tiles)
    owned[...] = jnp.dot(
        onehot[...].astype(BF16), tiles[...].astype(BF16), preferred_element_type=F32
    )
    hole_row = jnp.concatenate(
        [hole_v[...].astype(F32), jnp.zeros((1, TILE - n), F32)], axis=1
    ) if n < TILE else hole_v[...].astype(F32)
    first = lax.broadcasted_iota(jnp.int32, (CAP, TILE), 0) == 0
    hole_block = jnp.where(first, jnp.broadcast_to(hole_row, (CAP, TILE)), 0.0)

    def compose(d):
        def block(e):
            return owned[pl.ds(pl.multiple_of(e * CAP, CAP), CAP), :]

        low, high = lax.rem(d + n - 1, n), lax.rem(d + 1, n)
        send1[d] = jnp.concatenate(
            [block(low), block(d), block(high), hole_block], axis=0
        ).astype(BF16)

    pl.semaphore_wait(barrier, n - 1)

    def to_owner(d):
        compose(d)
        pltpu.make_async_remote_copy(
            src_ref=send1.at[d],
            dst_ref=recv1.at[me],
            send_sem=send1_sem,
            recv_sem=recv1_sem,
            device_id={"pair": d},
        ).start()

    to_peers(to_owner)
    compose(me)
    recv1[me] = send1[me]

    onehot_t[...] = onehot[...].T.astype(BF16)
    copy_direct.wait()
    copy_virt.wait()
    copy_screen.wait()
    copy_occ.wait()
    lay(direct_v, direct_t)

    def everything(send, recv, send_sem, recv_sem):
        return pltpu.make_async_remote_copy(
            src_ref=send.at[pl.ds(0, n - 1)],
            dst_ref=recv.at[pl.ds(0, n - 1)],
            send_sem=send_sem,
            recv_sem=recv_sem,
            device_id={"pair": lax.rem(me + 1, n)},
        )

    everything(send1, recv1, send1_sem, recv1_sem).wait_recv()

    recv1_f[...] = recv1[...].astype(F32).reshape(n * MSG, TILE)
    for j in range(3 * CAP):
        ext[j] = recv1_f[pl.ds(j, n, stride=MSG), :].astype(BF16)
    holes = recv1_f[pl.ds(3 * CAP, n, stride=MSG), :][:, :n].astype(BF16)

    for s in range(CAP):
        ladder_copies[s].wait()
        picked = jnp.concatenate([ext[screen[s, k]] for k in range(nq)], axis=1)
        ladder = jnp.dot(picked, ladder_v[s], preferred_element_type=F32)
        hole = jnp.dot(holes, ext[CAP + s], preferred_element_type=F32)
        coupled[pl.ds(s * n, n), :] = ladder + hole

    def split(i):
        send2[i] = coupled[pl.ds(i, CAP, stride=n), :]

    def to_row(d):
        split(d)
        pltpu.make_async_remote_copy(
            src_ref=send2.at[d],
            dst_ref=recv2.at[me],
            send_sem=send2_sem,
            recv_sem=recv2_sem,
            device_id={"pair": d},
        ).start()

    to_peers(to_row)
    split(me)
    recv2[me] = send2[me]
    everything(send2, recv2, send2_sem, recv2_sem).wait_recv()

    home = recv2[...].reshape(n * CAP, TILE).astype(BF16)
    sums = jnp.dot(onehot_t[...], home, preferred_element_type=F32)[:nt]
    out[...] = (direct_t[...] + sums) / (virt_v[...] - occ[0])
    everything(send1, recv1, send1_sem, recv1_sem).wait_send()
    everything(send2, recv2, send2_sem, recv2_sem).wait_send()


def shards(
    amplitudes, tile_counts, screen, ladder_ints, hole_ints, direct, occ_energy, virt_energy
):
    n = lax.axis_size("pair")
    nt = amplitudes.shape[1] // TILE
    nq = screen.shape[1]
    cols = -(-nt // TILE) * TILE
    if cols == nt:
        cols += TILE
    hbm = pl.BlockSpec(memory_space=pltpu.HBM)
    updated = pl.pallas_call(
        functools.partial(kernel, n, nt, nq),
        out_shape=jax.ShapeDtypeStruct((nt, TILE), F32),
        in_specs=[hbm] * 8,
        out_specs=pl.BlockSpec(memory_space=pltpu.VMEM),
        scratch_shapes=[
            pltpu.SMEM((n,), jnp.int32),
            pltpu.SMEM((CAP, nq), jnp.int32),
            pltpu.SMEM((1,), F32),
            pltpu.VMEM((1, nt * TILE), BF16),
            pltpu.VMEM((1, n), BF16),
            pltpu.VMEM((CAP, nq * TILE, TILE), BF16),
            pltpu.VMEM((1, nt * TILE), BF16),
            pltpu.VMEM((nt, TILE), F32),
            pltpu.VMEM((cols, TILE), F32),
            pltpu.VMEM((nt, TILE), F32),
            pltpu.VMEM((n * CAP, cols), F32),
            pltpu.VMEM((cols, n * CAP), BF16),
            pltpu.VMEM((n * CAP, TILE), F32),
            pltpu.VMEM((n, MSG, TILE), BF16),
            pltpu.VMEM((n, MSG, TILE), BF16),
            pltpu.VMEM((n * MSG, TILE), F32),
            pltpu.VMEM((3 * CAP, n, TILE), BF16),
            pltpu.VMEM((CAP * n, TILE), F32),
            pltpu.VMEM((n, CAP, TILE), F32),
            pltpu.VMEM((n, CAP, TILE), F32),
            pltpu.SemaphoreType.DMA((7,)),
            pltpu.SemaphoreType.DMA((CAP,)),
            pltpu.SemaphoreType.DMA,
            pltpu.SemaphoreType.DMA,
            pltpu.SemaphoreType.DMA,
            pltpu.SemaphoreType.DMA,
        ],
        compiler_params=pltpu.CompilerParams(
            collective_id=0, has_side_effects=True, vmem_limit_bytes=62 * 1024 * 1024
        ),
        cost_estimate=pl.CostEstimate(
            flops=2 * CAP * nq * TILE * TILE * n,
            bytes_accessed=CAP * nq * TILE * TILE * 2,
            transcendentals=0,
        ),
    )(
        tile_counts,
        screen,
        occ_energy,
        amplitudes,
        hole_ints,
        ladder_ints.reshape(CAP, nq * TILE, TILE),
        direct,
        virt_energy.reshape(nt, TILE),
    )
    return updated.reshape(1, nt * TILE)


def solution(mesh):
    return jax.shard_map(
        shards,
        mesh=mesh,
        in_specs=(
            P(("parts", "pair"), None),
            P("parts"),
            P(("parts", "pair"), None),
            P(("parts", "pair"), None, None, None),
            P(("parts", "pair"), None),
            P(("parts", "pair"), None),
            P(("parts", "pair")),
            P("parts"),
        ),
        out_specs=P(("parts", "pair"), None),
        check_vma=False,
    )
```

```python
import functools

import jax
import jax.numpy as jnp
from jax import lax
from jax.experimental import pallas as pl
from jax.experimental.pallas import tpu as pltpu
from jax.sharding import PartitionSpec as P

TILE = 128
CAP = 8
GROUP = 4
MSG = 32
F32 = jnp.float32
BF16 = jnp.bfloat16


def each(count, body):
    if count <= 64:
        for i in range(count):
            body(i)
    else:
        def step(i, carry):
            body(i)
            return carry

        lax.fori_loop(0, count, step, 0)


def far_first(n):
    if n % GROUP or n > 64:
        return None
    groups = n // GROUP
    ends = []
    for far in range(1, groups // 2 + 1):
        ends.append([groups - far] if 2 * far == groups else [groups - far, far])
    steps = [(far, near) for pair in ends for near in range(GROUP) for far in pair]
    return steps + [(0, near) for near in range(1, GROUP)]


def kernel(
    n,
    nt,
    nq,
    counts_hbm,
    screen_hbm,
    occ_hbm,
    amp_hbm,
    hole_hbm,
    ladder_hbm,
    direct_hbm,
    virt_hbm,
    out,
    counts,
    screen,
    occ,
    amp_v,
    hole_v,
    ladder_v,
    direct_v,
    virt_v,
    tiles,
    direct_t,
    onehot,
    onehot_t,
    owned,
    send1,
    recv1,
    recv1_f,
    ext,
    coupled,
    send2,
    recv2,
    in_sem,
    ladder_sem,
    send1_sem,
    recv1_sem,
    send2_sem,
    recv2_sem,
):
    me = lax.axis_index("pair")
    cols = onehot.shape[1]
    steps = far_first(n)

    def to_peers(body):
        if steps is None:
            each(n - 1, lambda t: body(lax.rem(me + 1 + t, n)))
        else:
            for far, near in steps:
                group = lax.rem(me // GROUP + far, n // GROUP)
                body(group * GROUP + lax.rem(me + near, GROUP))

    copy_amp = pltpu.make_async_copy(amp_hbm, amp_v, in_sem.at[0])
    copy_hole = pltpu.make_async_copy(hole_hbm, hole_v, in_sem.at[1])
    copy_direct = pltpu.make_async_copy(direct_hbm, direct_v, in_sem.at[2])
    copy_virt = pltpu.make_async_copy(virt_hbm, virt_v, in_sem.at[3])
    copy_counts = pltpu.make_async_copy(counts_hbm, counts, in_sem.at[4])
    copy_screen = pltpu.make_async_copy(screen_hbm, screen, in_sem.at[5])
    copy_occ = pltpu.make_async_copy(occ_hbm, occ, in_sem.at[6])
    copy_counts.start()
    copy_amp.start()
    copy_hole.start()

    barrier = pltpu.get_barrier_semaphore()

    def greet(t):
        pl.semaphore_signal(
            barrier, inc=1, device_id={"pair": lax.rem(me + 1 + t, n)}
        )

    each(n - 1, greet)

    ladder_copies = [
        pltpu.make_async_copy(ladder_hbm.at[s], ladder_v.at[s], ladder_sem.at[s])
        for s in range(CAP)
    ]
    for copy in ladder_copies:
        copy.start()
    copy_screen.start()
    copy_direct.start()
    copy_virt.start()
    copy_occ.start()

    lane = lax.broadcasted_iota(jnp.int32, (CAP, cols), 1)
    slot = lax.broadcasted_iota(jnp.int32, (CAP, cols), 0)

    def mark(e, offset):
        count = counts[e]
        hit = jnp.logical_and(lane == slot + offset, slot < count)
        row = e * CAP if isinstance(e, int) else pl.multiple_of(e * CAP, CAP)
        onehot[pl.ds(row, CAP), :] = jnp.where(hit, 1.0, 0.0).astype(F32)
        return offset + count

    copy_counts.wait()
    if n <= 64:
        offset = jnp.int32(0)
        for e in range(n):
            offset = mark(e, offset)
    else:
        lax.fori_loop(0, n, mark, jnp.int32(0))

    copy_amp.wait()
    copy_hole.wait()
    tiles[pl.ds(nt, cols - nt), :] = jnp.zeros((cols - nt, TILE), F32)

    def lay(source, target):
        def body(t):
            at = t * TILE if isinstance(t, int) else pl.multiple_of(t * TILE, TILE)
            target[pl.ds(t, 1), :] = source[:, pl.ds(at, TILE)].astype(F32)

        each(nt, body)

    lay(amp_v, tiles)
    owned[...] = jnp.dot(
        onehot[...].astype(BF16), tiles[...].astype(BF16), preferred_element_type=F32
    )
    hole_row = jnp.concatenate(
        [hole_v[...].astype(F32), jnp.zeros((1, TILE - n), F32)], axis=1
    ) if n < TILE else hole_v[...].astype(F32)
    first = lax.broadcasted_iota(jnp.int32, (CAP, TILE), 0) == 0
    hole_block = jnp.where(first, jnp.broadcast_to(hole_row, (CAP, TILE)), 0.0)

    def compose(d):
        def block(e):
            return owned[pl.ds(pl.multiple_of(e * CAP, CAP), CAP), :]

        low, high = lax.rem(d + n - 1, n), lax.rem(d + 1, n)
        send1[d] = jnp.concatenate(
            [block(low), block(d), block(high), hole_block], axis=0
        ).astype(BF16)

    pl.semaphore_wait(barrier, n - 1)

    def to_owner(d):
        compose(d)
        pltpu.make_async_remote_copy(
            src_ref=send1.at[d],
            dst_ref=recv1.at[me],
            send_sem=send1_sem,
            recv_sem=recv1_sem,
            device_id={"pair": d},
        ).start()

    to_peers(to_owner)
    compose(me)
    recv1[me] = send1[me]

    onehot_t[...] = onehot[...].T.astype(BF16)
    copy_direct.wait()
    copy_virt.wait()
    copy_screen.wait()
    copy_occ.wait()
    lay(direct_v, direct_t)

    def everything(send, recv, send_sem, recv_sem):
        return pltpu.make_async_remote_copy(
            src_ref=send.at[pl.ds(0, n - 1)],
            dst_ref=recv.at[pl.ds(0, n - 1)],
            send_sem=send_sem,
            recv_sem=recv_sem,
            device_id={"pair": lax.rem(me + 1, n)},
        )

    everything(send1, recv1, send1_sem, recv1_sem).wait_recv()

    recv1_f[...] = recv1[...].astype(F32).reshape(n * MSG, TILE)
    for j in range(3 * CAP):
        ext[j] = recv1_f[pl.ds(j, n, stride=MSG), :].astype(BF16)
    holes = recv1_f[pl.ds(3 * CAP, n, stride=MSG), :][:, :n].astype(BF16)

    for s in range(CAP):
        ladder_copies[s].wait()
        picked = jnp.concatenate([ext[screen[s, k]] for k in range(nq)], axis=1)
        ladder = jnp.dot(picked, ladder_v[s], preferred_element_type=F32)
        hole = jnp.dot(holes, ext[CAP + s], preferred_element_type=F32)
        coupled[pl.ds(s * n, n), :] = ladder + hole

    def split(i):
        send2[i] = coupled[pl.ds(i, CAP, stride=n), :]

    def to_row(d):
        split(d)
        pltpu.make_async_remote_copy(
            src_ref=send2.at[d],
            dst_ref=recv2.at[me],
            send_sem=send2_sem,
            recv_sem=recv2_sem,
            device_id={"pair": d},
        ).start()

    to_peers(to_row)
    split(me)
    recv2[me] = send2[me]
    everything(send2, recv2, send2_sem, recv2_sem).wait_recv()

    home = recv2[...].reshape(n * CAP, TILE).astype(BF16)
    sums = jnp.dot(onehot_t[...], home, preferred_element_type=F32)[:nt]
    out[...] = (direct_t[...] + sums) / (virt_v[...] - occ[0])
    everything(send1, recv1, send1_sem, recv1_sem).wait_send()
    everything(send2, recv2, send2_sem, recv2_sem).wait_send()


def shards(
    amplitudes, tile_counts, screen, ladder_ints, hole_ints, direct, occ_energy, virt_energy
):
    n = lax.axis_size("pair")
    nt = amplitudes.shape[1] // TILE
    nq = screen.shape[1]
    cols = -(-nt // TILE) * TILE
    if cols == nt:
        cols += TILE
    hbm = pl.BlockSpec(memory_space=pltpu.HBM)
    updated = pl.pallas_call(
        functools.partial(kernel, n, nt, nq),
        out_shape=jax.ShapeDtypeStruct((nt, TILE), F32),
        in_specs=[hbm] * 8,
        out_specs=pl.BlockSpec(memory_space=pltpu.VMEM),
        scratch_shapes=[
            pltpu.SMEM((n,), jnp.int32),
            pltpu.SMEM((CAP, nq), jnp.int32),
            pltpu.SMEM((1,), F32),
            pltpu.VMEM((1, nt * TILE), BF16),
            pltpu.VMEM((1, n), BF16),
            pltpu.VMEM((CAP, nq * TILE, TILE), BF16),
            pltpu.VMEM((1, nt * TILE), BF16),
            pltpu.VMEM((nt, TILE), F32),
            pltpu.VMEM((cols, TILE), F32),
            pltpu.VMEM((nt, TILE), F32),
            pltpu.VMEM((n * CAP, cols), F32),
            pltpu.VMEM((cols, n * CAP), BF16),
            pltpu.VMEM((n * CAP, TILE), F32),
            pltpu.VMEM((n, MSG, TILE), BF16),
            pltpu.VMEM((n, MSG, TILE), BF16),
            pltpu.VMEM((n * MSG, TILE), F32),
            pltpu.VMEM((3 * CAP, n, TILE), BF16),
            pltpu.VMEM((CAP * n, TILE), F32),
            pltpu.VMEM((n, CAP, TILE), F32),
            pltpu.VMEM((n, CAP, TILE), F32),
            pltpu.SemaphoreType.DMA((7,)),
            pltpu.SemaphoreType.DMA((CAP,)),
            pltpu.SemaphoreType.DMA,
            pltpu.SemaphoreType.DMA,
            pltpu.SemaphoreType.DMA,
            pltpu.SemaphoreType.DMA,
        ],
        compiler_params=pltpu.CompilerParams(
            collective_id=0, has_side_effects=True, vmem_limit_bytes=48 * 1024 * 1024
        ),
        cost_estimate=pl.CostEstimate(
            flops=2 * CAP * nq * TILE * TILE * n,
            bytes_accessed=CAP * nq * TILE * TILE * 2,
            transcendentals=0,
        ),
    )(
        *[
            operand
            if operand.size == 1
            else pltpu.with_memory_space_constraint(operand, pltpu.HBM)
            for operand in (
                tile_counts,
                screen,
                occ_energy,
                amplitudes,
                hole_ints,
                ladder_ints.reshape(CAP, nq * TILE, TILE),
                direct,
                virt_energy.reshape(nt, TILE),
            )
        ]
    )
    return updated.reshape(1, nt * TILE)


def solution(mesh):
    return jax.shard_map(
        shards,
        mesh=mesh,
        in_specs=(
            P(("parts", "pair"), None),
            P("parts"),
            P(("parts", "pair"), None),
            P(("parts", "pair"), None, None, None),
            P(("parts", "pair"), None),
            P(("parts", "pair"), None),
            P(("parts", "pair")),
            P("parts"),
        ),
        out_specs=P(("parts", "pair"), None),
        check_vma=False,
    )
```

```python
import functools

import jax
import jax.numpy as jnp
from jax import lax
from jax.experimental import pallas as pl
from jax.experimental.pallas import tpu as pltpu
from jax.sharding import PartitionSpec as P

TILE = 128
CAP = 8
GROUP = 4
MSG = 32
F32 = jnp.float32
BF16 = jnp.bfloat16


def each(count, body):
    if count <= 64:
        for i in range(count):
            body(i)
    else:
        def step(i, carry):
            body(i)
            return carry

        lax.fori_loop(0, count, step, 0)


def far_first(n):
    if n % GROUP or n > 64:
        return None
    groups = n // GROUP
    ends = []
    for far in range(1, groups // 2 + 1):
        ends.append([groups - far] if 2 * far == groups else [groups - far, far])
    steps = [(far, near) for pair in ends for near in range(GROUP) for far in pair]
    return steps + [(0, near) for near in range(1, GROUP)]


def kernel(
    n,
    nt,
    nq,
    counts_hbm,
    screen_hbm,
    occ_hbm,
    amp_hbm,
    hole_hbm,
    ladder_hbm,
    direct_hbm,
    virt_hbm,
    out,
    counts,
    screen,
    occ,
    amp_v,
    hole_v,
    ladder_v,
    direct_v,
    virt_v,
    tiles,
    direct_t,
    onehot,
    onehot_t,
    owned,
    send1,
    recv1,
    recv1_f,
    ext,
    coupled,
    send2,
    recv2,
    in_sem,
    ladder_sem,
    send1_sem,
    recv1_sem,
    send2_sem,
    recv2_sem,
):
    me = lax.axis_index("pair")
    cols = onehot.shape[1]
    steps = far_first(n)

    def to_peers(body):
        if steps is None:
            each(n - 1, lambda t: body(lax.rem(me + 1 + t, n)))
        else:
            for far, near in steps:
                group = lax.rem(me // GROUP + far, n // GROUP)
                body(group * GROUP + lax.rem(me + near, GROUP))

    copy_amp = pltpu.make_async_copy(amp_hbm, amp_v, in_sem.at[0])
    copy_hole = pltpu.make_async_copy(hole_hbm, hole_v, in_sem.at[1])
    copy_direct = pltpu.make_async_copy(direct_hbm, direct_v, in_sem.at[2])
    copy_virt = pltpu.make_async_copy(virt_hbm, virt_v, in_sem.at[3])
    copy_counts = pltpu.make_async_copy(counts_hbm, counts, in_sem.at[4])
    copy_screen = pltpu.make_async_copy(screen_hbm, screen, in_sem.at[5])
    copy_occ = pltpu.make_async_copy(occ_hbm, occ, in_sem.at[6])
    copy_counts.start()
    copy_amp.start()
    copy_hole.start()

    barrier = pltpu.get_barrier_semaphore()

    def greet(d):
        pl.semaphore_signal(barrier, inc=1, device_id={"pair": d})

    to_peers(greet)

    ladder_copies = [
        pltpu.make_async_copy(ladder_hbm.at[s], ladder_v.at[s], ladder_sem.at[s])
        for s in range(CAP)
    ]
    for copy in ladder_copies:
        copy.start()
    copy_screen.start()
    copy_direct.start()
    copy_virt.start()
    copy_occ.start()

    lane = lax.broadcasted_iota(jnp.int32, (CAP, cols), 1)
    slot = lax.broadcasted_iota(jnp.int32, (CAP, cols), 0)

    def mark(e, offset):
        count = counts[e]
        hit = jnp.logical_and(lane == slot + offset, slot < count)
        row = e * CAP if isinstance(e, int) else pl.multiple_of(e * CAP, CAP)
        onehot[pl.ds(row, CAP), :] = jnp.where(hit, 1.0, 0.0).astype(F32)
        return offset + count

    copy_counts.wait()
    if n <= 64:
        offset = jnp.int32(0)
        for e in range(n):
            offset = mark(e, offset)
    else:
        lax.fori_loop(0, n, mark, jnp.int32(0))

    copy_amp.wait()
    copy_hole.wait()
    tiles[pl.ds(nt, cols - nt), :] = jnp.zeros((cols - nt, TILE), F32)

    def lay(source, target):
        def body(t):
            at = t * TILE if isinstance(t, int) else pl.multiple_of(t * TILE, TILE)
            target[pl.ds(t, 1), :] = source[:, pl.ds(at, TILE)].astype(F32)

        each(nt, body)

    lay(amp_v, tiles)
    owned[...] = jnp.dot(
        onehot[...].astype(BF16), tiles[...].astype(BF16), preferred_element_type=F32
    )
    hole_row = jnp.concatenate(
        [hole_v[...].astype(F32), jnp.zeros((1, TILE - n), F32)], axis=1
    ) if n < TILE else hole_v[...].astype(F32)
    first = lax.broadcasted_iota(jnp.int32, (CAP, TILE), 0) == 0
    hole_block = jnp.where(first, jnp.broadcast_to(hole_row, (CAP, TILE)), 0.0)

    def compose(d):
        def block(e):
            return owned[pl.ds(pl.multiple_of(e * CAP, CAP), CAP), :]

        low, high = lax.rem(d + n - 1, n), lax.rem(d + 1, n)
        send1[d] = jnp.concatenate(
            [block(low), block(d), block(high), hole_block], axis=0
        ).astype(BF16)

    pl.semaphore_wait(barrier, n - 1)

    def to_owner(d):
        compose(d)
        pltpu.make_async_remote_copy(
            src_ref=send1.at[d],
            dst_ref=recv1.at[me],
            send_sem=send1_sem,
            recv_sem=recv1_sem,
            device_id={"pair": d},
        ).start()

    to_peers(to_owner)
    compose(me)
    recv1[me] = send1[me]

    onehot_t[...] = onehot[...].T.astype(BF16)
    copy_direct.wait()
    copy_virt.wait()
    copy_screen.wait()
    copy_occ.wait()
    lay(direct_v, direct_t)

    def everything(send, recv, send_sem, recv_sem):
        return pltpu.make_async_remote_copy(
            src_ref=send.at[pl.ds(0, n - 1)],
            dst_ref=recv.at[pl.ds(0, n - 1)],
            send_sem=send_sem,
            recv_sem=recv_sem,
            device_id={"pair": lax.rem(me + 1, n)},
        )

    everything(send1, recv1, send1_sem, recv1_sem).wait_recv()

    recv1_f[...] = recv1[...].astype(F32).reshape(n * MSG, TILE)
    for j in range(3 * CAP):
        ext[j] = recv1_f[pl.ds(j, n, stride=MSG), :].astype(BF16)
    holes = recv1_f[pl.ds(3 * CAP, n, stride=MSG), :][:, :n].astype(BF16)

    for s in range(CAP):
        ladder_copies[s].wait()
        picked = jnp.concatenate([ext[screen[s, k]] for k in range(nq)], axis=1)
        ladder = jnp.dot(picked, ladder_v[s], preferred_element_type=F32)
        hole = jnp.dot(holes, ext[CAP + s], preferred_element_type=F32)
        coupled[pl.ds(s * n, n), :] = ladder + hole

    def split(i):
        send2[i] = coupled[pl.ds(i, CAP, stride=n), :]

    def to_row(d):
        split(d)
        pltpu.make_async_remote_copy(
            src_ref=send2.at[d],
            dst_ref=recv2.at[me],
            send_sem=send2_sem,
            recv_sem=recv2_sem,
            device_id={"pair": d},
        ).start()

    to_peers(to_row)
    split(me)
    recv2[me] = send2[me]
    everything(send2, recv2, send2_sem, recv2_sem).wait_recv()

    home = recv2[...].reshape(n * CAP, TILE).astype(BF16)
    sums = jnp.dot(onehot_t[...], home, preferred_element_type=F32)[:nt]
    out[...] = (direct_t[...] + sums) / (virt_v[...] - occ[0])
    everything(send1, recv1, send1_sem, recv1_sem).wait_send()
    everything(send2, recv2, send2_sem, recv2_sem).wait_send()


def shards(
    amplitudes, tile_counts, screen, ladder_ints, hole_ints, direct, occ_energy, virt_energy
):
    n = lax.axis_size("pair")
    nt = amplitudes.shape[1] // TILE
    nq = screen.shape[1]
    cols = -(-nt // TILE) * TILE
    if cols == nt:
        cols += TILE
    hbm = pl.BlockSpec(memory_space=pltpu.HBM)
    updated = pl.pallas_call(
        functools.partial(kernel, n, nt, nq),
        out_shape=jax.ShapeDtypeStruct((nt, TILE), F32),
        in_specs=[hbm] * 8,
        out_specs=pl.BlockSpec(memory_space=pltpu.VMEM),
        scratch_shapes=[
            pltpu.SMEM((n,), jnp.int32),
            pltpu.SMEM((CAP, nq), jnp.int32),
            pltpu.SMEM((1,), F32),
            pltpu.VMEM((1, nt * TILE), BF16),
            pltpu.VMEM((1, n), BF16),
            pltpu.VMEM((CAP, nq * TILE, TILE), BF16),
            pltpu.VMEM((1, nt * TILE), BF16),
            pltpu.VMEM((nt, TILE), F32),
            pltpu.VMEM((cols, TILE), F32),
            pltpu.VMEM((nt, TILE), F32),
            pltpu.VMEM((n * CAP, cols), F32),
            pltpu.VMEM((cols, n * CAP), BF16),
            pltpu.VMEM((n * CAP, TILE), F32),
            pltpu.VMEM((n, MSG, TILE), BF16),
            pltpu.VMEM((n, MSG, TILE), BF16),
            pltpu.VMEM((n * MSG, TILE), F32),
            pltpu.VMEM((3 * CAP, n, TILE), BF16),
            pltpu.VMEM((CAP * n, TILE), F32),
            pltpu.VMEM((n, CAP, TILE), F32),
            pltpu.VMEM((n, CAP, TILE), F32),
            pltpu.SemaphoreType.DMA((7,)),
            pltpu.SemaphoreType.DMA((CAP,)),
            pltpu.SemaphoreType.DMA,
            pltpu.SemaphoreType.DMA,
            pltpu.SemaphoreType.DMA,
            pltpu.SemaphoreType.DMA,
        ],
        compiler_params=pltpu.CompilerParams(
            collective_id=0, has_side_effects=True, vmem_limit_bytes=48 * 1024 * 1024
        ),
        cost_estimate=pl.CostEstimate(
            flops=2 * CAP * nq * TILE * TILE * n,
            bytes_accessed=CAP * nq * TILE * TILE * 2,
            transcendentals=0,
        ),
    )(
        *[
            operand
            if operand.size == 1
            else pltpu.with_memory_space_constraint(operand, pltpu.HBM)
            for operand in (
                tile_counts,
                screen,
                occ_energy,
                amplitudes,
                hole_ints,
                ladder_ints.reshape(CAP, nq * TILE, TILE),
                direct,
                virt_energy.reshape(nt, TILE),
            )
        ]
    )
    return updated.reshape(1, nt * TILE)


def solution(mesh):
    return jax.shard_map(
        shards,
        mesh=mesh,
        in_specs=(
            P(("parts", "pair"), None),
            P("parts"),
            P(("parts", "pair"), None),
            P(("parts", "pair"), None, None, None),
            P(("parts", "pair"), None),
            P(("parts", "pair"), None),
            P(("parts", "pair")),
            P("parts"),
        ),
        out_specs=P(("parts", "pair"), None),
        check_vma=False,
    )
```

```python
import functools

import jax
import jax.numpy as jnp
from jax import lax
from jax.experimental import pallas as pl
from jax.experimental.pallas import tpu as pltpu
from jax.sharding import PartitionSpec as P

TILE = 128
CAP = 8
GROUP = 4
MSG = 32
F32 = jnp.float32
BF16 = jnp.bfloat16


def each(count, body):
    if count <= 64:
        for i in range(count):
            body(i)
    else:
        def step(i, carry):
            body(i)
            return carry

        lax.fori_loop(0, count, step, 0)


def far_first(n):
    if n % GROUP or n > 64:
        return None
    groups = n // GROUP
    ends = []
    for far in range(1, groups // 2 + 1):
        ends.append([groups - far] if 2 * far == groups else [groups - far, far])
    steps = [(far, near) for pair in ends for near in range(GROUP) for far in pair]
    return steps + [(0, near) for near in range(1, GROUP)]


def kernel(
    n,
    nt,
    nq,
    counts_hbm,
    screen_hbm,
    occ_hbm,
    amp_hbm,
    hole_hbm,
    ladder_hbm,
    direct_hbm,
    virt_hbm,
    out,
    counts,
    screen,
    occ,
    amp_v,
    hole_v,
    ladder_v,
    direct_v,
    virt_v,
    tiles,
    direct_t,
    onehot,
    onehot_t,
    owned,
    send1,
    recv1,
    recv1_f,
    ext,
    coupled,
    send2,
    recv2,
    in_sem,
    ladder_sem,
    send1_sem,
    recv1_sem,
    send2_sem,
    recv2_sem,
):
    me = lax.axis_index("pair")
    cols = onehot.shape[1]
    steps = far_first(n)

    def to_peers(body):
        if steps is None:
            each(n - 1, lambda t: body(lax.rem(me + 1 + t, n)))
        else:
            for far, near in steps:
                group = lax.rem(me // GROUP + far, n // GROUP)
                body(group * GROUP + lax.rem(me + near, GROUP))

    copy_amp = pltpu.make_async_copy(amp_hbm, amp_v, in_sem.at[0])
    copy_hole = pltpu.make_async_copy(hole_hbm, hole_v, in_sem.at[1])
    copy_direct = pltpu.make_async_copy(direct_hbm, direct_v, in_sem.at[2])
    copy_virt = pltpu.make_async_copy(virt_hbm, virt_v, in_sem.at[3])
    copy_counts = pltpu.make_async_copy(counts_hbm, counts, in_sem.at[4])
    copy_screen = pltpu.make_async_copy(screen_hbm, screen, in_sem.at[5])
    copy_occ = pltpu.make_async_copy(occ_hbm, occ, in_sem.at[6])
    copy_counts.start()
    copy_amp.start()
    copy_hole.start()

    barrier = pltpu.get_barrier_semaphore()

    def greet(d):
        pl.semaphore_signal(barrier, inc=1, device_id={"pair": d})

    to_peers(greet)

    ladder_copies = [
        pltpu.make_async_copy(ladder_hbm.at[s], ladder_v.at[s], ladder_sem.at[s])
        for s in range(CAP)
    ]

    lane = lax.broadcasted_iota(jnp.int32, (CAP, cols), 1)
    slot = lax.broadcasted_iota(jnp.int32, (CAP, cols), 0)

    def mark(e, offset):
        count = counts[e]
        hit = jnp.logical_and(lane == slot + offset, slot < count)
        row = e * CAP if isinstance(e, int) else pl.multiple_of(e * CAP, CAP)
        onehot[pl.ds(row, CAP), :] = jnp.where(hit, 1.0, 0.0).astype(F32)
        return offset + count

    copy_counts.wait()
    if n <= 64:
        offset = jnp.int32(0)
        for e in range(n):
            offset = mark(e, offset)
    else:
        lax.fori_loop(0, n, mark, jnp.int32(0))

    copy_amp.wait()
    copy_hole.wait()
    tiles[pl.ds(nt, cols - nt), :] = jnp.zeros((cols - nt, TILE), F32)

    def lay(source, target):
        def body(t):
            at = t * TILE if isinstance(t, int) else pl.multiple_of(t * TILE, TILE)
            target[pl.ds(t, 1), :] = source[:, pl.ds(at, TILE)].astype(F32)

        each(nt, body)

    lay(amp_v, tiles)
    owned[...] = jnp.dot(
        onehot[...].astype(BF16), tiles[...].astype(BF16), preferred_element_type=F32
    )
    hole_row = jnp.concatenate(
        [hole_v[...].astype(F32), jnp.zeros((1, TILE - n), F32)], axis=1
    ) if n < TILE else hole_v[...].astype(F32)
    first = lax.broadcasted_iota(jnp.int32, (CAP, TILE), 0) == 0
    hole_block = jnp.where(first, jnp.broadcast_to(hole_row, (CAP, TILE)), 0.0)

    def compose(d):
        def block(e):
            return owned[pl.ds(pl.multiple_of(e * CAP, CAP), CAP), :]

        low, high = lax.rem(d + n - 1, n), lax.rem(d + 1, n)
        send1[d] = jnp.concatenate(
            [block(low), block(d), block(high), hole_block], axis=0
        ).astype(BF16)

    pl.semaphore_wait(barrier, n - 1)

    def to_owner(d):
        compose(d)
        pltpu.make_async_remote_copy(
            src_ref=send1.at[d],
            dst_ref=recv1.at[me],
            send_sem=send1_sem,
            recv_sem=recv1_sem,
            device_id={"pair": d},
        ).start()

    to_peers(to_owner)
    for copy in ladder_copies:
        copy.start()
    copy_screen.start()
    copy_direct.start()
    copy_virt.start()
    copy_occ.start()
    compose(me)
    recv1[me] = send1[me]

    onehot_t[...] = onehot[...].T.astype(BF16)
    copy_direct.wait()
    copy_virt.wait()
    copy_screen.wait()
    copy_occ.wait()
    lay(direct_v, direct_t)

    def everything(send, recv, send_sem, recv_sem):
        return pltpu.make_async_remote_copy(
            src_ref=send.at[pl.ds(0, n - 1)],
            dst_ref=recv.at[pl.ds(0, n - 1)],
            send_sem=send_sem,
            recv_sem=recv_sem,
            device_id={"pair": lax.rem(me + 1, n)},
        )

    everything(send1, recv1, send1_sem, recv1_sem).wait_recv()

    recv1_f[...] = recv1[...].astype(F32).reshape(n * MSG, TILE)
    for j in range(3 * CAP):
        ext[j] = recv1_f[pl.ds(j, n, stride=MSG), :].astype(BF16)
    holes = recv1_f[pl.ds(3 * CAP, n, stride=MSG), :][:, :n].astype(BF16)

    for s in range(CAP):
        ladder_copies[s].wait()
        picked = jnp.concatenate([ext[screen[s, k]] for k in range(nq)], axis=1)
        ladder = jnp.dot(picked, ladder_v[s], preferred_element_type=F32)
        hole = jnp.dot(holes, ext[CAP + s], preferred_element_type=F32)
        coupled[pl.ds(s * n, n), :] = ladder + hole

    def split(i):
        send2[i] = coupled[pl.ds(i, CAP, stride=n), :]

    def to_row(d):
        split(d)
        pltpu.make_async_remote_copy(
            src_ref=send2.at[d],
            dst_ref=recv2.at[me],
            send_sem=send2_sem,
            recv_sem=recv2_sem,
            device_id={"pair": d},
        ).start()

    to_peers(to_row)
    split(me)
    recv2[me] = send2[me]
    everything(send2, recv2, send2_sem, recv2_sem).wait_recv()

    home = recv2[...].reshape(n * CAP, TILE).astype(BF16)
    sums = jnp.dot(onehot_t[...], home, preferred_element_type=F32)[:nt]
    out[...] = (direct_t[...] + sums) / (virt_v[...] - occ[0])
    everything(send1, recv1, send1_sem, recv1_sem).wait_send()
    everything(send2, recv2, send2_sem, recv2_sem).wait_send()


def shards(
    amplitudes, tile_counts, screen, ladder_ints, hole_ints, direct, occ_energy, virt_energy
):
    n = lax.axis_size("pair")
    nt = amplitudes.shape[1] // TILE
    nq = screen.shape[1]
    cols = -(-nt // TILE) * TILE
    if cols == nt:
        cols += TILE
    hbm = pl.BlockSpec(memory_space=pltpu.HBM)
    updated = pl.pallas_call(
        functools.partial(kernel, n, nt, nq),
        out_shape=jax.ShapeDtypeStruct((nt, TILE), F32),
        in_specs=[hbm] * 8,
        out_specs=pl.BlockSpec(memory_space=pltpu.VMEM),
        scratch_shapes=[
            pltpu.SMEM((n,), jnp.int32),
            pltpu.SMEM((CAP, nq), jnp.int32),
            pltpu.SMEM((1,), F32),
            pltpu.VMEM((1, nt * TILE), BF16),
            pltpu.VMEM((1, n), BF16),
            pltpu.VMEM((CAP, nq * TILE, TILE), BF16),
            pltpu.VMEM((1, nt * TILE), BF16),
            pltpu.VMEM((nt, TILE), F32),
            pltpu.VMEM((cols, TILE), F32),
            pltpu.VMEM((nt, TILE), F32),
            pltpu.VMEM((n * CAP, cols), F32),
            pltpu.VMEM((cols, n * CAP), BF16),
            pltpu.VMEM((n * CAP, TILE), F32),
            pltpu.VMEM((n, MSG, TILE), BF16),
            pltpu.VMEM((n, MSG, TILE), BF16),
            pltpu.VMEM((n * MSG, TILE), F32),
            pltpu.VMEM((3 * CAP, n, TILE), BF16),
            pltpu.VMEM((CAP * n, TILE), F32),
            pltpu.VMEM((n, CAP, TILE), F32),
            pltpu.VMEM((n, CAP, TILE), F32),
            pltpu.SemaphoreType.DMA((7,)),
            pltpu.SemaphoreType.DMA((CAP,)),
            pltpu.SemaphoreType.DMA,
            pltpu.SemaphoreType.DMA,
            pltpu.SemaphoreType.DMA,
            pltpu.SemaphoreType.DMA,
        ],
        compiler_params=pltpu.CompilerParams(
            collective_id=0, has_side_effects=True, vmem_limit_bytes=48 * 1024 * 1024
        ),
        cost_estimate=pl.CostEstimate(
            flops=2 * CAP * nq * TILE * TILE * n,
            bytes_accessed=CAP * nq * TILE * TILE * 2,
            transcendentals=0,
        ),
    )(
        *[
            operand
            if operand.size == 1
            else pltpu.with_memory_space_constraint(operand, pltpu.HBM)
            for operand in (
                tile_counts,
                screen,
                occ_energy,
                amplitudes,
                hole_ints,
                ladder_ints.reshape(CAP, nq * TILE, TILE),
                direct,
                virt_energy.reshape(nt, TILE),
            )
        ]
    )
    return updated.reshape(1, nt * TILE)


def solution(mesh):
    return jax.shard_map(
        shards,
        mesh=mesh,
        in_specs=(
            P(("parts", "pair"), None),
            P("parts"),
            P(("parts", "pair"), None),
            P(("parts", "pair"), None, None, None),
            P(("parts", "pair"), None),
            P(("parts", "pair"), None),
            P(("parts", "pair")),
            P("parts"),
        ),
        out_specs=P(("parts", "pair"), None),
        check_vma=False,
    )
```
